32 devices in a mesh: group: 2 (over y), expert: 4 (over z), tensor: 4 (over x, core).
Axes of the slice: x: 2, y: 2, z: 4, core: 2. Of those that a mesh axis runs over, the one named last changes fastest.
Arguments:
- q_absorbed: bfloat16 [1024, 36864], P(('group', 'expert'), 'tensor'), parts along dimension 0, may hold values from -14 to 14
- kv_latent: bfloat16 [1024, 576], P(('group', 'expert')), parts along dimension 0, may hold values from -4 to 4
- w_values: bfloat16 [64, 512, 128], P('tensor'), may hold values from -1 to 1
- w_out: bfloat16 [8192, 7168], P('tensor', 'expert'), may hold values from -0.0625 to 0.0625
- layer_input: bfloat16 [1024, 7168], P(('group', 'expert')), parts along dimension 0, may hold values from -40 to 40
- norm_gain: float32 [7168], replicated, may hold values from 0.1 to 1.9
- predicted: int32 [1024, 8], P(('group', 'expert')), parts along dimension 0, may hold values from 0 to 15, as said below
- actual: int32 [1024, 8], P(('group', 'expert')), parts along dimension 0, may hold values from 0 to 15, as said below
- gates: float32 [1024, 8], P(('group', 'expert')), parts along dimension 0, may hold values from 0.1 to 1
- w_gate: bfloat16 [16, 7168, 1024], P('expert', 'tensor'), may hold values from -0.0625 to 0.0625
- w_up: bfloat16 [16, 7168, 1024], P('expert', 'tensor'), may hold values from -0.0625 to 0.0625
- w_down: bfloat16 [16, 1024, 7168], P('expert', None, 'tensor'), may hold values from -0.1875 to 0.1875
Outputs:
- attended: bfloat16 [1024, 7168], P(('group', 'expert'), 'tensor'), parts along dimension 0
- mixture: bfloat16 [1024, 7168], P(('group', 'expert'), 'tensor'), parts along dimension 0
- missed: float32 [1024], P(('group', 'expert')), parts along dimension 0
The draws below stay inside these ranges and needn't reach their ends.
There are 2 independent parts, one for each index of `group`. The reference program is written for one: setup_inputs(seed, part) draws one part's arguments, and reference() takes and returns one part's arrays. A program takes and returns all parts, laid end to end along the dimension named above; an argument that names none is the same for every part. Nothing has to cross between parts.
Inputs may be any that keep to these rules, and one draw needn't show every extreme that they name: `predicted`: each row names 8 different experts. In each aligned block of 128 rows (the rows of one index of expert) at most 80 rows name the same expert, and in every draw some expert is named by exactly 80 rows of every block. `actual`: each row names 8 different experts. In each aligned block of 128 rows (the rows of one index of expert) at most 12 rows name a given expert that the same row of predicted does not name, and in every draw some expert reaches 12 such rows in every block.
All inputs are finite; a program needn't handle non-finite values.
Results may differ from the reference program's by a relative error of at most 0.023.
Values may be sent and summed in bfloat16 or wider, within the bound.
A program may use at most 128 MiB of HBM per device.

```python
import math
import jax
import jax.numpy as jnp
from jax import lax

D = 7168
LAT = 512
ROPE = 64
VDIM = 128
TOP = 8
HEADS = 64
FF = 1024
ACTIVE_EXPERTS = 16
T_DEV = 128
QK = 576
SEQUENCE_TOKENS = 512
CAP = 80
CAP_C = 12
N_EXPERT = 4
N_TENSOR = 4


def draw_kv_latent(key, part):
    base = jnp.clip(jax.random.normal(jax.random.fold_in(key, 32), (SEQUENCE_TOKENS, QK), jnp.float32), -4.0, 4.0)
    return base.astype(jnp.bfloat16)


def draw_q_absorbed(key, part):
    base = jnp.clip(1.15 * jax.random.normal(jax.random.fold_in(key, 33), (SEQUENCE_TOKENS, HEADS, QK), jnp.float32), -4.6, 4.6)
    return base.reshape(SEQUENCE_TOKENS, HEADS * QK).astype(jnp.bfloat16)


def draw_layer_input(key, part):
    row_scale = jnp.exp(jax.random.uniform(jax.random.fold_in(key, 51), (SEQUENCE_TOKENS, 1), jnp.float32, -1.15, 1.15))
    col_scale = jnp.exp(jax.random.uniform(jax.random.fold_in(key, 52), (1, D), jnp.float32, -1.15, 1.15))
    base = jnp.clip(jax.random.normal(jax.random.fold_in(key, 53), (SEQUENCE_TOKENS, D), jnp.float32), -4.0, 4.0)
    return (base * row_scale * col_scale).astype(jnp.bfloat16)


def route_plan(key):
    blocks = SEQUENCE_TOKENS // T_DEV
    spread = 3 * T_DEV // 4
    order = jax.random.permutation(jax.random.fold_in(key, 40), ACTIVE_EXPERTS)
    flag_markers = jax.random.randint(jax.random.fold_in(key, 41), (2,), 0, ACTIVE_EXPERTS)
    block_keys = jax.random.split(jax.random.fold_in(key, 42), blocks)
    rank_positions = jax.vmap(lambda block_key: jax.random.permutation(block_key, T_DEV))(block_keys).reshape(SEQUENCE_TOKENS)
    block_displacement = jnp.repeat(jax.random.randint(jax.random.fold_in(key, 43), (blocks,), 0, 2), T_DEV)
    sudden_batch = flag_markers[0] + block_displacement + jax.random.randint(jax.random.fold_in(key, 44), (SEQUENCE_TOKENS,), 0, 4)
    spread_flag = rank_positions < spread
    start_displacement = jnp.where(spread_flag, rank_positions % ACTIVE_EXPERTS, sudden_batch) % ACTIVE_EXPERTS
    near = (start_displacement == flag_markers[1] % ACTIVE_EXPERTS) | (start_displacement == (flag_markers[1] + ACTIVE_EXPERTS - 1) % ACTIVE_EXPERTS)
    random_move = jax.random.randint(jax.random.fold_in(key, 45), (SEQUENCE_TOKENS,), 0, 3)
    moved = jnp.where(spread_flag, jnp.where(near, 2, random_move), 0)
    steps = jnp.arange(TOP)
    guess = order[(start_displacement[:, None] + steps[None, :]) % ACTIVE_EXPERTS]
    truth = order[(start_displacement[:, None] + moved[:, None] + steps[None, :]) % ACTIVE_EXPERTS]
    return (guess.astype(jnp.int32), truth.astype(jnp.int32))


def draw_predicted(key, part):
    return route_plan(key)[0]


def draw_actual(key, part):
    return route_plan(key)[1]


def block_scale(key, shape, shards, least, top_value):
    gain, own = 1.0, jax.random.fold_in(key, 6)
    for position, shards_of in shards:
        steps = jnp.exp(jax.random.uniform(jax.random.fold_in(own, position), (shards_of,), jnp.float32, least / len(shards), top_value / len(shards)))
        gain = gain * jnp.repeat(steps, shape[position] // shards_of).reshape([-1 if axis == position else 1 for axis in range(len(shape))])
    return gain


def normal_values(rng, shape, scale, reach, cuts=(), kind=jnp.bfloat16):
    drawn = jax.random.normal(rng, shape, jnp.float32) * scale
    if len(cuts) > 0:
        drawn = block_scale(rng, shape, cuts, -0.22, 0.18) * drawn
    return jnp.clip(drawn, min=-reach, max=reach).astype(kind)


def setup_inputs(seed: int = 0, part: int = 0) -> dict:
    key_of = jax.random.split(jax.random.key(seed), 13)
    own_keys = jax.random.split(jax.random.fold_in(key_of[12], part), 13)
    return {
        "q_absorbed": draw_q_absorbed(jax.random.fold_in(jax.random.fold_in(key_of[12], part), 71), part),
        "kv_latent": draw_kv_latent(jax.random.fold_in(jax.random.fold_in(key_of[12], part), 71), part),
        "w_values": normal_values(key_of[2], (HEADS, LAT, VDIM), (LAT // 16) ** -0.5, 1.0, ((0, 4),)),
        "w_out": normal_values(key_of[3], (HEADS * VDIM, D), (HEADS * VDIM) ** -0.5, 0.0625, ((0, 4), (1, 4))),
        "layer_input": draw_layer_input(jax.random.fold_in(jax.random.fold_in(key_of[12], part), 71), part),
        "norm_gain": jnp.clip(1.0 + 0.18 * jax.random.normal(key_of[5], (D,), jnp.float32), 0.1, 1.9),
        "predicted": draw_predicted(jax.random.fold_in(jax.random.fold_in(key_of[12], part), 71), part),
        "actual": draw_actual(jax.random.fold_in(jax.random.fold_in(key_of[12], part), 71), part),
        "gates": jnp.clip(jnp.exp(math.log(1.0) - 2.3025851 * jax.random.uniform(own_keys[8], (SEQUENCE_TOKENS, TOP), jnp.float32) ** block_scale(own_keys[8], (SEQUENCE_TOKENS, TOP), ((0, 4),), -0.2, 0.2)), 0.1, 1.0),
        "w_gate": normal_values(key_of[9], (ACTIVE_EXPERTS, D, FF), D ** -0.5, 0.0625, ((0, 4), (1, 4))),
        "w_up": normal_values(key_of[10], (ACTIVE_EXPERTS, D, FF), D ** -0.5, 0.0625, ((0, 4), (1, 4))),
        "w_down": normal_values(key_of[11], (ACTIVE_EXPERTS, FF, D), FF ** -0.5, 0.1875, ((0, 4), (2, 4))),
    }


EPS = 1e-06

def head_attention(query, weight, kv_latent, visible, scale):
    scores = jnp.dot(query, kv_latent.T, preferred_element_type=jnp.float32) * scale
    masked = jnp.where(visible, scores, -jnp.inf)
    largest = lax.optimization_barrier(jnp.max(masked, axis=1, keepdims=True))
    expo = jnp.exp(masked - largest)
    denominator = lax.optimization_barrier(jnp.sum(expo, axis=1, keepdims=True))
    weights = expo.astype(jnp.bfloat16)
    latent = jnp.dot(weights, kv_latent[:, :LAT], preferred_element_type=jnp.float32) / denominator
    latent = latent.astype(jnp.bfloat16)
    return jnp.dot(latent, weight, preferred_element_type=jnp.float32).astype(jnp.bfloat16)

def range_sum(pieces, weight):
    blocks = weight.reshape(N_TENSOR, D // N_TENSOR, FF).astype(jnp.float32)
    terms = jnp.einsum('ntd,tdf->tnf', pieces, blocks)
    rounded = lax.optimization_barrier(terms.astype(jnp.bfloat16))
    return lax.optimization_barrier(jnp.sum(rounded.astype(jnp.float32), axis=0))

def expert_rows(picked_rows, weight_gate, weight_up, weight_down):
    count = picked_rows.shape[0]
    pieces = picked_rows.reshape(count, N_TENSOR, D // N_TENSOR).astype(jnp.float32)
    gate_pre = range_sum(pieces, weight_gate)
    up_pre = range_sum(pieces, weight_up)
    act = (jax.nn.silu(gate_pre) * up_pre).astype(jnp.bfloat16)
    return jnp.dot(act, weight_down, preferred_element_type=jnp.float32).astype(jnp.bfloat16)

def reference(q_absorbed, kv_latent, w_values, w_out, layer_input, norm_gain, predicted, actual, gates, w_gate, w_up, w_down):
    scale = (VDIM + ROPE) ** (-0.5)
    positions = jnp.arange(SEQUENCE_TOKENS, dtype=jnp.int32)
    visible = positions[:, None] >= positions[None, :]
    queries = jnp.transpose(q_absorbed.reshape(SEQUENCE_TOKENS, HEADS, QK), (1, 0, 2))

    def one_head(pair):
        return head_attention(pair[0], pair[1], kv_latent, visible, scale)
    heads_out = lax.map(one_head, (queries, w_values))
    heads_flat = jnp.transpose(heads_out, (1, 0, 2)).reshape(SEQUENCE_TOKENS, HEADS * VDIM)
    attended = jnp.dot(heads_flat, w_out, preferred_element_type=jnp.float32).astype(jnp.bfloat16)
    features = layer_input.astype(jnp.float32)
    inverse = lax.rsqrt(lax.optimization_barrier(jnp.mean(features * features, axis=1, keepdims=True)) + EPS)
    normed = (features * inverse * norm_gain).astype(jnp.bfloat16)
    matched = jnp.any(predicted[:, None, :] == actual[:, :, None], axis=2)
    missed = lax.optimization_barrier(jnp.sum(jnp.where(matched, 0.0, gates), axis=1))
    flat_true = actual.reshape(-1)
    flat_gate = gates.reshape(-1)
    capacity = N_EXPERT * (CAP + CAP_C)

    def add_expert(running, item):
        index, weight_gate, weight_up, weight_down = item
        chosen = flat_true == index
        picked = jnp.nonzero(chosen, size=capacity, fill_value=0)[0].astype(jnp.int32)
        valid = jnp.arange(capacity, dtype=jnp.int32) < jnp.sum(chosen.astype(jnp.int32))
        token_index = (picked // TOP).astype(jnp.int32)
        result = expert_rows(normed[token_index], weight_gate, weight_up, weight_down).astype(jnp.float32)
        weight = jnp.where(valid, flat_gate[picked], 0.0)
        return (running.at[token_index].add(weight[:, None] * result), None)
    mixture, _ = lax.scan(add_expert, jnp.zeros((SEQUENCE_TOKENS, D), jnp.float32), (jnp.arange(ACTIVE_EXPERTS, dtype=jnp.int32), w_gate, w_up, w_down))
    return (attended, mixture.astype(jnp.bfloat16), missed)
```

```python
import functools

import jax
import jax.numpy as jnp
from jax import lax
from jax.sharding import PartitionSpec as P

ROPE = 64
VDIM = 128
CAP = 80
CAP_C = 12


EPS = 1e-06
FLOOR = -1e30


def bits_of(count):
    return count.bit_length() - 1


def share_of(index, count):
    share = 0
    for bit in range(bits_of(count)):
        share = share * 2 + ((index >> bit) & 1)
    return share


def halve(part, dim, bit, count):
    own = (lax.axis_index("tensor") >> bit) & 1
    half = part.shape[dim] // 2
    send = lax.dynamic_slice_in_dim(part, (1 - own) * half, half, dim).astype(jnp.bfloat16)
    keep = lax.dynamic_slice_in_dim(part, own * half, half, dim).astype(jnp.float32)
    got = lax.ppermute(send, "tensor", [(i, i ^ (1 << bit)) for i in range(count)])
    return keep + got.astype(jnp.float32)


def reduce_halving(part, dim, count):
    for bit in range(bits_of(count)):
        part = halve(part, dim, bit, count)
    return part


def gather_doubling(part, dim, count):
    for bit in reversed(range(bits_of(count))):
        own = (lax.axis_index("tensor") >> bit) & 1
        got = lax.ppermute(part, "tensor", [(i, i ^ (1 << bit)) for i in range(count)])
        first = jnp.where(own == 0, part, got)
        second = jnp.where(own == 0, got, part)
        part = jnp.concatenate([first, second], axis=dim)
    return part


def attention(q_absorbed, kv_all, w_values):
    token_count = q_absorbed.shape[0]
    heads_here = w_values.shape[0]
    latent_width = w_values.shape[1]
    key_width = kv_all.shape[1]
    scale = (VDIM + ROPE) ** (-0.5)
    queries = q_absorbed.reshape(token_count * heads_here, key_width)
    query_pos = jnp.repeat(
        lax.axis_index("expert") * token_count + jnp.arange(token_count, dtype=jnp.int32),
        heads_here,
    )
    scores = (
        lax.dot_general(
            queries, kv_all, (((1,), (1,)), ((), ())), preferred_element_type=jnp.float32
        )
        * scale
    )
    key_pos = jnp.arange(kv_all.shape[0], dtype=jnp.int32)
    visible = query_pos[:, None] >= key_pos[None, :]
    masked = jnp.where(visible, scores, FLOOR)
    largest = jnp.max(masked, axis=1)
    expo = jnp.where(visible, jnp.exp(masked - largest[:, None]), 0.0)
    denominator = jnp.sum(expo, axis=1)
    accum = jnp.dot(
        expo.astype(jnp.bfloat16), kv_all[:, :latent_width], preferred_element_type=jnp.float32
    )
    latent = (
        (accum / denominator[:, None])
        .astype(jnp.bfloat16)
        .reshape(token_count, heads_here, latent_width)
    )
    heads_out = jnp.einsum(
        "thc,hcv->thv", latent, w_values, preferred_element_type=jnp.float32
    ).astype(jnp.bfloat16)
    return heads_out.reshape(token_count, heads_here * w_values.shape[2])


def body(
    n_expert,
    n_tensor,
    q_absorbed,
    kv_latent,
    w_values,
    w_out,
    layer_input,
    norm_gain,
    predicted,
    actual,
    gates,
    w_gate,
    w_up,
    w_down,
):
    local, slice_width, hidden = w_gate.shape
    experts = local * n_expert
    paired = n_tensor & (n_tensor - 1) == 0

    matches = predicted[:, None, :] == actual[:, :, None]
    matched = jnp.any(matches, axis=2)
    missed = jnp.sum(jnp.where(matched, 0.0, gates), axis=1)
    names = jnp.arange(experts, dtype=jnp.int32)
    gate_map = jnp.sum(
        jnp.where(actual[:, :, None] == names[None, None, :], gates[:, :, None], 0.0), axis=1
    )
    gate_all = lax.all_gather(gate_map, "expert", axis=0, tiled=True)
    kv_all = lax.all_gather(kv_latent, "expert", axis=0, tiled=True)

    first_col = lax.axis_index("tensor") * slice_width
    features = layer_input.astype(jnp.float32)
    inverse = lax.rsqrt(jnp.mean(features * features, axis=1, keepdims=True) + EPS)
    mine = lax.dynamic_slice_in_dim(layer_input, first_col, slice_width, 1).astype(jnp.float32)
    gain_mine = lax.dynamic_slice_in_dim(norm_gain, first_col, slice_width, 0)
    normed = (mine * inverse * gain_mine).astype(jnp.bfloat16)
    normed_all = lax.all_gather(normed, "expert", axis=0, tiled=True)

    heads_out = attention(q_absorbed, kv_all, w_values)
    heads_all = lax.all_gather(heads_out, "expert", axis=0, tiled=True)

    tokens = normed_all.shape[0]
    depth = n_expert * (CAP + CAP_C)
    gate_here = lax.dynamic_slice_in_dim(
        gate_all, lax.axis_index("expert") * local, local, 1
    )
    chosen = gate_here > 0.0
    order = jnp.arange(tokens, dtype=jnp.int32)
    lower = (order[:, None] >= order[None, :]).astype(jnp.bfloat16)
    place = jnp.dot(lower, chosen.astype(jnp.bfloat16), preferred_element_type=jnp.float32)
    place = jnp.where(chosen, place.astype(jnp.int32) - 1, -1).T
    row_ids = jnp.arange(depth, dtype=jnp.int32)
    picks = place[:, None, :] == row_ids[None, :, None]
    row_gate = jnp.sum(jnp.where(picks, gate_here.T[:, None, :], 0.0), axis=2)
    picks = picks.astype(jnp.bfloat16)

    outs = []
    for e in range(local):
        rows = jnp.dot(picks[e], normed_all, preferred_element_type=jnp.float32).astype(
            jnp.bfloat16
        )
        gate_part = jnp.dot(rows, w_gate[e], preferred_element_type=jnp.float32)
        up_part = jnp.dot(rows, w_up[e], preferred_element_type=jnp.float32)
        gate_part, up_part = gate_part.astype(jnp.bfloat16), up_part.astype(jnp.bfloat16)
        if paired:
            gate_share = reduce_halving(gate_part, 1, n_tensor)
            up_share = reduce_halving(up_part, 1, n_tensor)
        else:
            gate_share = lax.psum_scatter(gate_part, "tensor", scatter_dimension=1, tiled=True)
            up_share = lax.psum_scatter(up_part, "tensor", scatter_dimension=1, tiled=True)
            gate_share = gate_share.astype(jnp.float32)
            up_share = up_share.astype(jnp.float32)
        act_part = (jax.nn.silu(gate_share) * up_share).astype(jnp.bfloat16)
        if paired:
            act = gather_doubling(act_part, 1, n_tensor)
        else:
            act = lax.all_gather(act_part, "tensor", axis=1, tiled=True)
        out = jnp.dot(act, w_down[e], preferred_element_type=jnp.float32)
        outs.append((out * row_gate[e][:, None]).astype(jnp.bfloat16))
    partial_mix = lax.dot_general(
        picks.reshape(local * depth, tokens),
        jnp.concatenate(outs, axis=0),
        (((0,), (0,)), ((), ())),
        preferred_element_type=jnp.float32,
    ).astype(jnp.bfloat16)
    mixture = lax.psum_scatter(partial_mix, "expert", scatter_dimension=0, tiled=True)

    partial_cols = jnp.dot(heads_all, w_out, preferred_element_type=jnp.float32).astype(
        jnp.bfloat16
    )
    if paired and n_expert == n_tensor:
        summed = reduce_halving(partial_cols, 0, n_tensor).astype(jnp.bfloat16)
        attended = lax.ppermute(
            summed,
            ("expert", "tensor"),
            [
                (e * n_tensor + t, share_of(t, n_tensor) * n_tensor + e)
                for e in range(n_expert)
                for t in range(n_tensor)
            ],
        )
    else:
        partial_rows = lax.all_to_all(
            partial_cols, "expert", split_axis=0, concat_axis=1, tiled=True
        )
        attended = lax.psum_scatter(partial_rows, "tensor", scatter_dimension=1, tiled=True)
    return (attended, mixture, missed)


def solution(mesh):
    placed = (
        P(("group", "expert"), "tensor"),
        P(("group", "expert"), None),
        P("tensor", None, None),
        P("tensor", "expert"),
        P(("group", "expert"), None),
        P(),
        P(("group", "expert"), None),
        P(("group", "expert"), None),
        P(("group", "expert"), None),
        P("expert", "tensor", None),
        P("expert", "tensor", None),
        P("expert", None, "tensor"),
    )
    return jax.shard_map(
        functools.partial(body, mesh.shape["expert"], mesh.shape["tensor"]),
        mesh=mesh,
        in_specs=placed,
        out_specs=(
            P(("group", "expert"), "tensor"),
            P(("group", "expert"), "tensor"),
            P(("group", "expert")),
        ),
        check_vma=False,
    )
```

```python
import functools

import jax
import jax.numpy as jnp
from jax import lax
from jax.experimental import pallas as pl
from jax.experimental.pallas import tpu as pltpu
from jax.sharding import PartitionSpec as P

ROPE = 64
VDIM = 128
CAP = 80
CAP_C = 12


EPS = 1e-06
FLOOR = -1e30


def bits_of(count):
    return count.bit_length() - 1


def share_of(index, count):
    share = 0
    for bit in range(bits_of(count)):
        share = share * 2 + ((index >> bit) & 1)
    return share


def halve(part, dim, bit, count):
    own = (lax.axis_index("tensor") >> bit) & 1
    half = part.shape[dim] // 2
    send = lax.dynamic_slice_in_dim(part, (1 - own) * half, half, dim).astype(jnp.bfloat16)
    keep = lax.dynamic_slice_in_dim(part, own * half, half, dim).astype(jnp.float32)
    got = lax.ppermute(send, "tensor", [(i, i ^ (1 << bit)) for i in range(count)])
    return keep + got.astype(jnp.float32)


def reduce_halving(part, dim, count):
    for bit in range(bits_of(count)):
        part = halve(part, dim, bit, count)
    return part


def gather_doubling(part, dim, count):
    for bit in reversed(range(bits_of(count))):
        own = (lax.axis_index("tensor") >> bit) & 1
        got = lax.ppermute(part, "tensor", [(i, i ^ (1 << bit)) for i in range(count)])
        first = jnp.where(own == 0, part, got)
        second = jnp.where(own == 0, got, part)
        part = jnp.concatenate([first, second], axis=dim)
    return part


def attention(q_absorbed, kv_all, w_values):
    token_count = q_absorbed.shape[0]
    heads_here = w_values.shape[0]
    latent_width = w_values.shape[1]
    key_width = kv_all.shape[1]
    scale = (VDIM + ROPE) ** (-0.5)
    queries = q_absorbed.reshape(token_count * heads_here, key_width)
    query_pos = jnp.repeat(
        lax.axis_index("expert") * token_count + jnp.arange(token_count, dtype=jnp.int32),
        heads_here,
    )
    scores = (
        lax.dot_general(
            queries, kv_all, (((1,), (1,)), ((), ())), preferred_element_type=jnp.float32
        )
        * scale
    )
    key_pos = jnp.arange(kv_all.shape[0], dtype=jnp.int32)
    visible = query_pos[:, None] >= key_pos[None, :]
    masked = jnp.where(visible, scores, FLOOR)
    largest = jnp.max(masked, axis=1)
    expo = jnp.where(visible, jnp.exp(masked - largest[:, None]), 0.0)
    denominator = jnp.sum(expo, axis=1)
    accum = jnp.dot(
        expo.astype(jnp.bfloat16), kv_all[:, :latent_width], preferred_element_type=jnp.float32
    )
    latent = (
        (accum / denominator[:, None])
        .astype(jnp.bfloat16)
        .reshape(token_count, heads_here, latent_width)
    )
    heads_out = jnp.einsum(
        "thc,hcv->thv", latent, w_values, preferred_element_type=jnp.float32
    ).astype(jnp.bfloat16)
    return heads_out.reshape(token_count, heads_here * w_values.shape[2])

MESH = pl.DeviceIdType.MESH


def experts_kernel(
    picks_ref,
    picks_t_ref,
    row_gate_ref,
    normed_ref,
    w_gate_ref,
    w_up_ref,
    w_down_ref,
    out_ref,
    gate_buf,
    up_buf,
    down_buf,
    rows,
    for_core,
    own_half,
    from_core,
    for_x,
    own_quarter,
    from_x,
    act,
    total,
    weight_sem,
    down_sem,
    core_send,
    core_recv,
    x_send,
    x_recv,
    act_x_send,
    act_x_recv,
    act_core_send,
    act_core_recv,
):
    local = picks_ref.shape[0]
    quarter = own_quarter.shape[3]
    width = normed_ref.shape[1]
    tile = 256
    me = lax.axis_index("tensor")
    core = lax.rem(me, 2)
    side = me // 2
    core_peer = side * 2 + 1 - core
    x_peer = (1 - side) * 2 + core
    mine = core * 2 + side

    def weight_copies(e):
        slot = lax.rem(e, 2)
        return (
            pltpu.make_async_copy(w_gate_ref.at[e], gate_buf.at[slot], weight_sem.at[0, slot]),
            pltpu.make_async_copy(w_up_ref.at[e], up_buf.at[slot], weight_sem.at[1, slot]),
        )

    def down_copy(e):
        slot = lax.rem(e, 2)
        return pltpu.make_async_copy(w_down_ref.at[e], down_buf.at[slot], down_sem.at[slot])

    def remote(src, dst, send, recv, peer):
        return pltpu.make_async_remote_copy(
            src_ref=src,
            dst_ref=dst,
            send_sem=send,
            recv_sem=recv,
            device_id={"tensor": peer},
            device_id_type=MESH,
        )

    def core_copy(e):
        return remote(
            for_core.at[e], from_core.at[e], core_send.at[e], core_recv.at[e], core_peer
        )

    def x_copy(e):
        return remote(for_x.at[e], from_x.at[e], x_send.at[e], x_recv.at[e], x_peer)

    def act_x_copy(e):
        part = act.at[e, mine]
        return remote(part, part, act_x_send.at[e], act_x_recv.at[e], x_peer)

    def act_core_copy(e):
        part = act.at[e, pl.ds(core * 2, 2)]
        return remote(part, part, act_core_send.at[e], act_core_recv.at[e], core_peer)

    for copy in weight_copies(0):
        copy.start()
    down_copy(0).start()
    barrier = pltpu.get_barrier_semaphore()
    for peer in (core_peer, x_peer):
        pl.semaphore_signal(barrier, inc=1, device_id={"tensor": peer}, device_id_type=MESH)
    pl.semaphore_wait(barrier, 2)
    total[...] = jnp.zeros_like(total)

    def multiply(e):
        slot = lax.rem(e, 2)

        @pl.when(e + 1 < local)
        def _():
            for copy in weight_copies(e + 1):
                copy.start()

        @pl.loop(0, width // tile)
        def _(j):
            cols = pl.ds(pl.multiple_of(j * tile, tile), tile)
            rows[:, cols] = jnp.dot(
                picks_ref[e], normed_ref[:, cols], preferred_element_type=jnp.float32
            ).astype(jnp.bfloat16)

        for copy in weight_copies(e):
            copy.wait()
        for half, target in ((1 - core, for_core), (core, own_half)):
            for k, x_half in enumerate((1 - side, side)):
                first = pl.multiple_of((half * 2 + x_half) * quarter, quarter)
                cols = pl.ds(first, quarter)
                for m, buf in enumerate((gate_buf, up_buf)):
                    target[e, 2 * k + m] = jnp.dot(
                        rows[...], buf[slot, :, cols], preferred_element_type=jnp.float32
                    ).astype(jnp.bfloat16)
            if target is for_core:
                core_copy(e).start()

    def add_core(e):
        core_copy(e).wait()
        for k in range(2):
            for_x[e, k] = (
                own_half[e, k].astype(jnp.float32) + from_core[e, k].astype(jnp.float32)
            ).astype(jnp.bfloat16)
        x_copy(e).start()
        for k in range(2):
            own_quarter[e, k] = own_half[e, 2 + k].astype(jnp.float32) + from_core[
                e, 2 + k
            ].astype(jnp.float32)

    def activate(e):
        x_copy(e).wait()
        gate = own_quarter[e, 0] + from_x[e, 0].astype(jnp.float32)
        up = own_quarter[e, 1] + from_x[e, 1].astype(jnp.float32)
        act[e, mine] = (gate / (1.0 + jnp.exp(-gate)) * up).astype(jnp.bfloat16)
        act_x_copy(e).start()

    def pass_on(e):
        act_x_copy(e).wait()
        act_core_copy(e).start()

    def project(e):
        slot = lax.rem(e, 2)

        @pl.when(e + 1 < local)
        def _():
            down_copy(e + 1).start()

        act_core_copy(e).wait()
        down_copy(e).wait()

        @pl.loop(0, width // tile)
        def _(j):
            cols = pl.ds(pl.multiple_of(j * tile, tile), tile)
            out = jnp.zeros((act.shape[2], tile), jnp.float32)
            for q in range(act.shape[1]):
                out += jnp.dot(
                    act[e, q],
                    down_buf[slot, q * quarter : (q + 1) * quarter, cols],
                    preferred_element_type=jnp.float32,
                )
            out = (out * row_gate_ref[e]).astype(jnp.bfloat16)
            total[:, cols] += jnp.dot(picks_t_ref[e], out, preferred_element_type=jnp.float32)

    @pl.loop(0, local + 4)
    def _(step):
        @pl.when((step >= 1) & (step < local + 1))
        def _():
            add_core(step - 1)

        @pl.when(step < local)
        def _():
            multiply(step)

        @pl.when((step >= 2) & (step < local + 2))
        def _():
            activate(step - 2)

        @pl.when((step >= 3) & (step < local + 3))
        def _():
            pass_on(step - 3)

        @pl.when(step >= 4)
        def _():
            project(step - 4)

    out_ref[...] = total[...].astype(out_ref.dtype)


def run_experts(picks, picks_t, row_gate, normed_all, w_gate, w_up, w_down):
    local, depth, tokens = picks.shape
    _, width, hidden = w_gate.shape
    quarter = hidden // 4
    bf16, f32 = jnp.bfloat16, jnp.float32
    dma = pltpu.SemaphoreType.DMA
    vmem = pl.BlockSpec(memory_space=pltpu.VMEM)
    hbm = pl.BlockSpec(memory_space=pl.ANY)
    return pl.pallas_call(
        experts_kernel,
        out_shape=jax.ShapeDtypeStruct((tokens, width), bf16),
        in_specs=[vmem] * 4 + [hbm] * 3,
        out_specs=vmem,
        scratch_shapes=[
            pltpu.VMEM((2, width, hidden), bf16),
            pltpu.VMEM((2, width, hidden), bf16),
            pltpu.VMEM((2, hidden, width), bf16),
            pltpu.VMEM((depth, width), bf16),
            pltpu.VMEM((local, 4, depth, quarter), bf16),
            pltpu.VMEM((local, 4, depth, quarter), bf16),
            pltpu.VMEM((local, 4, depth, quarter), bf16),
            pltpu.VMEM((local, 2, depth, quarter), bf16),
            pltpu.VMEM((local, 2, depth, quarter), f32),
            pltpu.VMEM((local, 2, depth, quarter), bf16),
            pltpu.VMEM((local, 4, depth, quarter), bf16),
            pltpu.VMEM((tokens, width), f32),
            dma((2, 2)),
            dma((2,)),
        ]
        + [dma((local,))] * 8,
        compiler_params=pltpu.CompilerParams(
            collective_id=0, has_side_effects=True, vmem_limit_bytes=60 * 1024 * 1024
        ),
        cost_estimate=pl.CostEstimate(
            flops=2 * local * depth * width * (3 * hidden + 2 * tokens),
            bytes_accessed=3 * local * width * hidden * 2,
            transcendentals=local * depth * quarter,
        ),
    )(picks, picks_t, row_gate, normed_all, w_gate, w_up, w_down)


def body(
    n_expert,
    n_tensor,
    q_absorbed,
    kv_latent,
    w_values,
    w_out,
    layer_input,
    norm_gain,
    predicted,
    actual,
    gates,
    w_gate,
    w_up,
    w_down,
):
    local, slice_width, hidden = w_gate.shape
    experts = local * n_expert
    paired = n_tensor & (n_tensor - 1) == 0

    matches = predicted[:, None, :] == actual[:, :, None]
    matched = jnp.any(matches, axis=2)
    missed = jnp.sum(jnp.where(matched, 0.0, gates), axis=1)
    names = jnp.arange(experts, dtype=jnp.int32)
    gate_map = jnp.sum(
        jnp.where(actual[:, :, None] == names[None, None, :], gates[:, :, None], 0.0), axis=1
    )
    gate_terms, rest = [], gate_map
    for _ in range(3):
        term = lax.reduce_precision(rest, 8, 7)
        gate_terms.append(term.astype(jnp.bfloat16))
        rest = rest - term
    fill = -(kv_latent.shape[1] + 3 * experts) % 128
    gate_terms.append(jnp.zeros((gate_map.shape[0], fill), jnp.bfloat16))
    mixed = lax.all_gather(
        jnp.concatenate([kv_latent, *gate_terms], axis=1), "expert", axis=0, tiled=True
    )
    key_width = kv_latent.shape[1]
    kv_all = mixed[:, :key_width]
    gate_all = sum(
        mixed[:, key_width + i * experts : key_width + (i + 1) * experts].astype(jnp.float32)
        for i in range(3)
    )

    first_col = lax.axis_index("tensor") * slice_width
    features = layer_input.astype(jnp.float32)
    inverse = lax.rsqrt(jnp.mean(features * features, axis=1, keepdims=True) + EPS)
    mine = lax.dynamic_slice_in_dim(layer_input, first_col, slice_width, 1).astype(jnp.float32)
    gain_mine = lax.dynamic_slice_in_dim(norm_gain, first_col, slice_width, 0)
    normed = (mine * inverse * gain_mine).astype(jnp.bfloat16)
    normed_all = lax.all_gather(normed, "expert", axis=0, tiled=True)

    heads_out = attention(q_absorbed, kv_all, w_values)
    heads_all = lax.all_gather(heads_out, "expert", axis=0, tiled=True)
    normed_all, heads_out = lax.optimization_barrier((normed_all, heads_out))

    tokens = normed_all.shape[0]
    depth = n_expert * (CAP + CAP_C)
    gate_here = lax.dynamic_slice_in_dim(
        gate_all, lax.axis_index("expert") * local, local, 1
    )
    chosen = gate_here > 0.0
    order = jnp.arange(tokens, dtype=jnp.int32)
    lower = (order[:, None] >= order[None, :]).astype(jnp.bfloat16)
    place = jnp.dot(lower, chosen.astype(jnp.bfloat16), preferred_element_type=jnp.float32)
    place = jnp.where(chosen, place.astype(jnp.int32) - 1, -1).T
    row_ids = jnp.arange(depth, dtype=jnp.int32)
    picks = place[:, None, :] == row_ids[None, :, None]
    row_gate = jnp.sum(jnp.where(picks, gate_here.T[:, None, :], 0.0), axis=2)
    picks = picks.astype(jnp.bfloat16)

    if n_tensor == 4 and hidden % 1024 == 0 and slice_width % 256 == 0 and depth % 16 == 0:
        partial_mix = run_experts(
            picks,
            picks.transpose(0, 2, 1),
            row_gate[:, :, None],
            normed_all,
            w_gate,
            w_up,
            w_down,
        )
    else:
        outs = []
        for e in range(local):
            rows = jnp.dot(picks[e], normed_all, preferred_element_type=jnp.float32).astype(
                jnp.bfloat16
            )
            gate_part = jnp.dot(rows, w_gate[e], preferred_element_type=jnp.float32)
            up_part = jnp.dot(rows, w_up[e], preferred_element_type=jnp.float32)
            gate_part, up_part = gate_part.astype(jnp.bfloat16), up_part.astype(jnp.bfloat16)
            if paired:
                gate_share = reduce_halving(gate_part, 1, n_tensor)
                up_share = reduce_halving(up_part, 1, n_tensor)
            else:
                gate_share = lax.psum_scatter(gate_part, "tensor", scatter_dimension=1, tiled=True)
                up_share = lax.psum_scatter(up_part, "tensor", scatter_dimension=1, tiled=True)
                gate_share = gate_share.astype(jnp.float32)
                up_share = up_share.astype(jnp.float32)
            act_part = (jax.nn.silu(gate_share) * up_share).astype(jnp.bfloat16)
            if paired:
                act = gather_doubling(act_part, 1, n_tensor)
            else:
                act = lax.all_gather(act_part, "tensor", axis=1, tiled=True)
            out = jnp.dot(act, w_down[e], preferred_element_type=jnp.float32)
            outs.append((out * row_gate[e][:, None]).astype(jnp.bfloat16))
        partial_mix = lax.dot_general(
            picks.reshape(local * depth, tokens),
            jnp.concatenate(outs, axis=0),
            (((0,), (0,)), ((), ())),
            preferred_element_type=jnp.float32,
        ).astype(jnp.bfloat16)
    mixture = lax.psum_scatter(partial_mix, "expert", scatter_dimension=0, tiled=True)

    partial_cols = jnp.dot(heads_all, w_out, preferred_element_type=jnp.float32).astype(
        jnp.bfloat16
    )
    if paired and n_expert == n_tensor:
        summed = reduce_halving(partial_cols, 0, n_tensor).astype(jnp.bfloat16)
        attended = lax.ppermute(
            summed,
            ("expert", "tensor"),
            [
                (e * n_tensor + t, share_of(t, n_tensor) * n_tensor + e)
                for e in range(n_expert)
                for t in range(n_tensor)
            ],
        )
    else:
        partial_rows = lax.all_to_all(
            partial_cols, "expert", split_axis=0, concat_axis=1, tiled=True
        )
        attended = lax.psum_scatter(partial_rows, "tensor", scatter_dimension=1, tiled=True)
    return (attended, mixture, missed)


def solution(mesh):
    placed = (
        P(("group", "expert"), "tensor"),
        P(("group", "expert"), None),
        P("tensor", None, None),
        P("tensor", "expert"),
        P(("group", "expert"), None),
        P(),
        P(("group", "expert"), None),
        P(("group", "expert"), None),
        P(("group", "expert"), None),
        P("expert", "tensor", None),
        P("expert", "tensor", None),
        P("expert", None, "tensor"),
    )
    return jax.shard_map(
        functools.partial(body, mesh.shape["expert"], mesh.shape["tensor"]),
        mesh=mesh,
        in_specs=placed,
        out_specs=(
            P(("group", "expert"), "tensor"),
            P(("group", "expert"), "tensor"),
            P(("group", "expert")),
        ),
        check_vma=False,
    )
```

```python
import functools

import jax
import jax.numpy as jnp
from jax import lax
from jax.experimental import pallas as pl
from jax.experimental.pallas import tpu as pltpu
from jax.sharding import PartitionSpec as P

ROPE = 64
VDIM = 128
CAP = 80
CAP_C = 12


EPS = 1e-06
FLOOR = -1e30


def bits_of(count):
    return count.bit_length() - 1


def share_of(index, count):
    share = 0
    for bit in range(bits_of(count)):
        share = share * 2 + ((index >> bit) & 1)
    return share


def halve(part, dim, bit, count):
    own = (lax.axis_index("tensor") >> bit) & 1
    half = part.shape[dim] // 2
    send = lax.dynamic_slice_in_dim(part, (1 - own) * half, half, dim).astype(jnp.bfloat16)
    keep = lax.dynamic_slice_in_dim(part, own * half, half, dim).astype(jnp.float32)
    got = lax.ppermute(send, "tensor", [(i, i ^ (1 << bit)) for i in range(count)])
    return keep + got.astype(jnp.float32)


def reduce_halving(part, dim, count):
    for bit in range(bits_of(count)):
        part = halve(part, dim, bit, count)
    return part


def gather_doubling(part, dim, count):
    for bit in reversed(range(bits_of(count))):
        own = (lax.axis_index("tensor") >> bit) & 1
        got = lax.ppermute(part, "tensor", [(i, i ^ (1 << bit)) for i in range(count)])
        first = jnp.where(own == 0, part, got)
        second = jnp.where(own == 0, got, part)
        part = jnp.concatenate([first, second], axis=dim)
    return part


def place_rows(gate, depth):
    tokens = gate.shape[1]
    chosen = gate > 0.0
    order = jnp.arange(tokens, dtype=jnp.int32)
    upper = (order[:, None] <= order[None, :]).astype(jnp.bfloat16)
    place = jnp.dot(chosen.astype(jnp.bfloat16), upper, preferred_element_type=jnp.float32)
    place = jnp.where(chosen, place.astype(jnp.int32) - 1, -1)
    row_ids = jnp.arange(depth, dtype=jnp.int32)
    picks = place[:, None, :] == row_ids[None, :, None]
    row_gate = jnp.sum(jnp.where(picks, gate[:, None, :], 0.0), axis=2)
    return picks.astype(jnp.bfloat16), row_gate


def attention(q_absorbed, kv_all, w_values):
    token_count = q_absorbed.shape[0]
    heads_here = w_values.shape[0]
    latent_width = w_values.shape[1]
    key_width = kv_all.shape[1]
    scale = (VDIM + ROPE) ** (-0.5)
    queries = q_absorbed.reshape(token_count * heads_here, key_width)
    query_pos = jnp.repeat(
        lax.axis_index("expert") * token_count + jnp.arange(token_count, dtype=jnp.int32),
        heads_here,
    )
    scores = (
        lax.dot_general(
            queries, kv_all, (((1,), (1,)), ((), ())), preferred_element_type=jnp.float32
        )
        * scale
    )
    key_pos = jnp.arange(kv_all.shape[0], dtype=jnp.int32)
    visible = query_pos[:, None] >= key_pos[None, :]
    masked = jnp.where(visible, scores, FLOOR)
    largest = jnp.max(masked, axis=1)
    expo = jnp.where(visible, jnp.exp(masked - largest[:, None]), 0.0)
    denominator = jnp.sum(expo, axis=1)
    accum = jnp.dot(
        expo.astype(jnp.bfloat16), kv_all[:, :latent_width], preferred_element_type=jnp.float32
    )
    latent = (
        (accum / denominator[:, None])
        .astype(jnp.bfloat16)
        .reshape(token_count, heads_here, latent_width)
    )
    heads_out = jnp.einsum(
        "thc,hcv->thv", latent, w_values, preferred_element_type=jnp.float32
    ).astype(jnp.bfloat16)
    return heads_out.reshape(token_count, heads_here * w_values.shape[2])

MESH = pl.DeviceIdType.MESH


def fused_kernel(
    picks_ref,
    picks_t_ref,
    row_gate_ref,
    normed_ref,
    heads_ref,
    w_gate_ref,
    w_up_ref,
    w_down_ref,
    w_out_ref,
    attended_ref,
    mixture_ref,
    gate_buf,
    up_buf,
    down_buf,
    out_buf,
    rows,
    for_core,
    own_half,
    from_core,
    for_x,
    own_quarter,
    from_x,
    act,
    total,
    mix_out,
    mix_in,
    heads,
    cols_part,
    cols_core,
    cols_for_x,
    cols_from_x,
    cols_out,
    cols_in,
    weight_sem,
    down_sem,
    out_sem,
    core_send,
    core_recv,
    x_send,
    x_recv,
    act_x_send,
    act_x_recv,
    act_core_send,
    act_core_recv,
    mix_send,
    mix_recv,
    heads_send,
    heads_recv,
    cols_send,
    cols_recv,
):
    steps = picks_ref.shape[0]
    local = w_gate_ref.shape[0]
    blocks, token_count, _ = heads.shape
    quarter = own_quarter.shape[3]
    width = normed_ref.shape[1]
    tile = 256
    z = lax.axis_index("expert")
    me = lax.axis_index("tensor")
    core = lax.rem(me, 2)
    side = me // 2
    core_peer = side * 2 + 1 - core
    x_peer = (1 - side) * 2 + core
    mine = core * 2 + side
    stays = (mine == z) & (z == me)

    def remote(src, dst, send, recv, peer):
        return pltpu.make_async_remote_copy(
            src_ref=src,
            dst_ref=dst,
            send_sem=send,
            recv_sem=recv,
            device_id=peer,
            device_id_type=MESH,
        )

    def weight_copies(s):
        slot, e = lax.rem(s, 2), lax.rem(s, local)
        return (
            pltpu.make_async_copy(w_gate_ref.at[e], gate_buf.at[slot], weight_sem.at[0, slot]),
            pltpu.make_async_copy(w_up_ref.at[e], up_buf.at[slot], weight_sem.at[1, slot]),
        )

    def down_copy(s):
        slot, e = lax.rem(s, 2), lax.rem(s, local)
        return pltpu.make_async_copy(w_down_ref.at[e], down_buf.at[slot], down_sem.at[slot])

    def out_copy(j):
        slot = lax.rem(j, 2)
        cols = pl.ds(pl.multiple_of(j * tile, tile), tile)
        return pltpu.make_async_copy(w_out_ref.at[:, cols], out_buf.at[slot], out_sem.at[slot])

    def core_copy(s):
        return remote(
            for_core.at[lax.rem(s, 2)],
            from_core.at[s],
            core_send.at[s],
            core_recv.at[s],
            {"tensor": core_peer},
        )

    def x_copy(s):
        return remote(
            for_x.at[lax.rem(s, 2)], from_x.at[s], x_send.at[s], x_recv.at[s], {"tensor": x_peer}
        )

    def act_x_copy(s):
        part = act.at[s, mine]
        return remote(part, part, act_x_send.at[s], act_x_recv.at[s], {"tensor": x_peer})

    def act_core_copy(s):
        part = act.at[s, pl.ds(core * 2, 2)]
        return remote(part, part, act_core_send.at[s], act_core_recv.at[s], {"tensor": core_peer})

    def heads_copy(k):
        peer = lax.rem(z + k, blocks)
        return remote(
            heads_ref, heads.at[z], heads_send.at[k - 1], heads_recv.at[z], {"expert": peer}
        )

    def heads_arrival(k):
        source = lax.rem(z + k, blocks)
        return remote(
            heads_ref, heads.at[source], heads_send.at[k - 1], heads_recv.at[source], {"expert": source}
        )

    def cols_core_copy():
        return remote(
            cols_part.at[pl.ds((1 - core) * 2, 2)],
            cols_core,
            cols_send.at[0],
            cols_recv.at[0],
            {"tensor": core_peer},
        )

    def cols_x_copy():
        return remote(
            cols_for_x, cols_from_x, cols_send.at[1], cols_recv.at[1], {"tensor": x_peer}
        )

    def cols_final_copy():
        return remote(
            cols_out,
            cols_in,
            cols_send.at[2],
            cols_recv.at[2],
            {"expert": mine, "tensor": z},
        )

    def mix_target(half, i):
        return half + i * (blocks - 1 - 2 * half)

    def mix_copy(half, i):
        return remote(
            mix_out.at[half, i],
            mix_in.at[z],
            mix_send.at[half, i],
            mix_recv.at[z],
            {"expert": mix_target(half, i)},
        )

    def mix_arrival(source):
        return remote(
            mix_out.at[0, 0],
            mix_in.at[source],
            mix_send.at[0, 0],
            mix_recv.at[source],
            {"expert": source},
        )

    for copy in weight_copies(0):
        copy.start()
    down_copy(0).start()
    barrier = pltpu.get_barrier_semaphore()

    def greet(peer):
        pl.semaphore_signal(barrier, inc=1, device_id=peer, device_id_type=MESH)

    greet({"tensor": core_peer})
    greet({"tensor": x_peer})
    for k in range(1, blocks):
        greet({"expert": lax.rem(z + k, blocks)})

    @pl.when(jnp.logical_not(stays))
    def _():
        greet({"expert": mine, "tensor": z})
        greet({"expert": me, "tensor": lax.rem(z, 2) * 2 + z // 2})

    @pl.when(stays)
    def _():
        pl.semaphore_wait(barrier, 1 + blocks)

    @pl.when(jnp.logical_not(stays))
    def _():
        pl.semaphore_wait(barrier, 3 + blocks)

    for k in range(1, blocks):
        heads_copy(k).start()
    heads[z] = heads_ref[...]

    def multiply(s):
        slot = lax.rem(s, 2)
        half_tokens = picks_ref.shape[2]
        first_token = pl.multiple_of(s // local * half_tokens, half_tokens)

        @pl.when(s + 1 < steps)
        def _():
            for copy in weight_copies(s + 1):
                copy.start()

        @pl.loop(0, width // tile)
        def _(j):
            cols = pl.ds(pl.multiple_of(j * tile, tile), tile)
            rows[:, cols] = jnp.dot(
                picks_ref[s],
                normed_ref[pl.ds(first_token, half_tokens), cols],
                preferred_element_type=jnp.float32,
            ).astype(jnp.bfloat16)

        for copy in weight_copies(s):
            copy.wait()
        for half, target in ((1 - core, for_core), (core, own_half)):
            for k, x_half in enumerate((1 - side, side)):
                first = pl.multiple_of((half * 2 + x_half) * quarter, quarter)
                cols = pl.ds(first, quarter)
                for m, buf in enumerate((gate_buf, up_buf)):
                    target[slot, 2 * k + m] = jnp.dot(
                        rows[...], buf[slot, :, cols], preferred_element_type=jnp.float32
                    ).astype(jnp.bfloat16)
            if target is for_core:
                core_copy(s).start()

    def add_core(s):
        slot = lax.rem(s, 2)
        core_copy(s).wait()
        for k in range(2):
            for_x[slot, k] = (
                own_half[slot, k].astype(jnp.float32) + from_core[s, k].astype(jnp.float32)
            ).astype(jnp.bfloat16)
        x_copy(s).start()
        for k in range(2):
            own_quarter[slot, k] = own_half[slot, 2 + k].astype(jnp.float32) + from_core[
                s, 2 + k
            ].astype(jnp.float32)

    def activate(s):
        slot = lax.rem(s, 2)
        x_copy(s).wait()
        gate = own_quarter[slot, 0] + from_x[s, 0].astype(jnp.float32)
        up = own_quarter[slot, 1] + from_x[s, 1].astype(jnp.float32)
        act[s, mine] = (gate / (1.0 + jnp.exp(-gate)) * up).astype(jnp.bfloat16)
        act_x_copy(s).start()

    def pass_on(s):
        act_x_copy(s).wait()
        act_core_copy(s).start()

    def project(s):
        slot = lax.rem(s, 2)

        @pl.when(s + 1 < steps)
        def _():
            down_copy(s + 1).start()

        @pl.when(lax.rem(s, local) == 0)
        def _():
            total[...] = jnp.zeros_like(total)

        act_core_copy(s).wait()
        down_copy(s).wait()

        @pl.loop(0, width // tile)
        def _(j):
            cols = pl.ds(pl.multiple_of(j * tile, tile), tile)
            out = jnp.zeros((act.shape[2], tile), jnp.float32)
            for q in range(act.shape[1]):
                out += jnp.dot(
                    act[s, q],
                    down_buf[slot, q * quarter : (q + 1) * quarter, cols],
                    preferred_element_type=jnp.float32,
                )
            out = (out * row_gate_ref[s]).astype(jnp.bfloat16)
            total[:, cols] += jnp.dot(picks_t_ref[s], out, preferred_element_type=jnp.float32)

        @pl.when(lax.rem(s, local) == local - 1)
        def _():
            half = s // local
            for i in range(2):
                mix_out[half, i] = total[i * token_count : (i + 1) * token_count, :].astype(
                    jnp.bfloat16
                )

                @pl.when(mix_target(half, i) != z)
                def _():
                    mix_copy(half, i).start()

                @pl.when(mix_target(half, i) == z)
                def _():
                    mix_in[z] = mix_out[half, i]

    def multiply_heads():
        out_copy(0).start()
        for k in range(1, blocks):
            heads_copy(k).wait_send()
            heads_arrival(k).wait_recv()

        @pl.loop(0, width // tile)
        def _(j):
            @pl.when(j + 1 < width // tile)
            def _():
                out_copy(j + 1).start()

            out_copy(j).wait()
            cols = pl.ds(pl.multiple_of(j * tile, tile), tile)
            for b in range(blocks // 2):
                part = heads[2 * b : 2 * b + 2].reshape(2 * token_count, heads.shape[2])
                part = jnp.dot(
                    part, out_buf[lax.rem(j, 2)], preferred_element_type=jnp.float32
                ).astype(jnp.bfloat16)
                cols_part[2 * b : 2 * b + 2, :, cols] = part.reshape(2, token_count, tile)

        cols_core_copy().start()

    def add_cols_core():
        cols_core_copy().wait()
        cols_for_x[...] = (
            cols_part[core * 2 + 1 - side].astype(jnp.float32)
            + cols_core[1 - side].astype(jnp.float32)
        ).astype(jnp.bfloat16)
        cols_x_copy().start()

    def add_cols_x():
        cols_x_copy().wait()
        cols_out[...] = (
            cols_part[mine].astype(jnp.float32)
            + cols_core[side].astype(jnp.float32)
            + cols_from_x[...].astype(jnp.float32)
        ).astype(jnp.bfloat16)

        @pl.when(jnp.logical_not(stays))
        def _():
            cols_final_copy().start()

    @pl.loop(0, steps + 4)
    def _(step):
        @pl.when((step >= 1) & (step < steps + 1))
        def _():
            add_core(step - 1)

        @pl.when(step < steps)
        def _():
            multiply(step)

        @pl.when((step >= 2) & (step < steps + 2))
        def _():
            activate(step - 2)

        @pl.when((step >= 3) & (step < steps + 3))
        def _():
            pass_on(step - 3)

        @pl.when(step >= 4)
        def _():
            project(step - 4)

        @pl.when(step == steps - 2)
        def _():
            multiply_heads()

        @pl.when(step == steps - 1)
        def _():
            add_cols_core()

        @pl.when(step == steps)
        def _():
            add_cols_x()

    @pl.when(jnp.logical_not(stays))
    def _():
        cols_final_copy().wait()
        attended_ref[...] = cols_in[...]

    @pl.when(stays)
    def _():
        attended_ref[...] = cols_out[...]

    for half in range(2):
        for i in range(2):

            @pl.when(mix_target(half, i) != z)
            def _():
                mix_copy(half, i).wait_send()

    for source in range(blocks):

        @pl.when(z != source)
        def _():
            mix_arrival(source).wait_recv()

    mixed = mix_in[0].astype(jnp.float32)
    for source in range(1, blocks):
        mixed += mix_in[source].astype(jnp.float32)
    mixture_ref[...] = mixed.astype(jnp.bfloat16)


def run_fused(picks, picks_t, row_gate, normed_all, heads_out, w_gate, w_up, w_down, w_out):
    steps, depth, half_tokens = picks.shape
    local, width, hidden = w_gate.shape
    token_count, head_width = heads_out.shape
    blocks = 4
    quarter = hidden // 4
    bf16, f32 = jnp.bfloat16, jnp.float32
    dma = pltpu.SemaphoreType.DMA
    vmem = pl.BlockSpec(memory_space=pltpu.VMEM)
    hbm = pl.BlockSpec(memory_space=pl.ANY)
    block = (token_count, width)
    return pl.pallas_call(
        fused_kernel,
        out_shape=[jax.ShapeDtypeStruct(block, bf16)] * 2,
        in_specs=[vmem] * 5 + [hbm] * 4,
        out_specs=[vmem] * 2,
        scratch_shapes=[
            pltpu.VMEM((2, width, hidden), bf16),
            pltpu.VMEM((2, width, hidden), bf16),
            pltpu.VMEM((2, hidden, width), bf16),
            pltpu.VMEM((2, head_width, 256), bf16),
            pltpu.VMEM((depth, width), bf16),
            pltpu.VMEM((2, 4, depth, quarter), bf16),
            pltpu.VMEM((2, 4, depth, quarter), bf16),
            pltpu.VMEM((steps, 4, depth, quarter), bf16),
            pltpu.VMEM((2, 2, depth, quarter), bf16),
            pltpu.VMEM((2, 2, depth, quarter), f32),
            pltpu.VMEM((steps, 2, depth, quarter), bf16),
            pltpu.VMEM((steps, 4, depth, quarter), bf16),
            pltpu.VMEM((half_tokens, width), f32),
            pltpu.VMEM((2, 2, *block), bf16),
            pltpu.VMEM((blocks, *block), bf16),
            pltpu.VMEM((blocks, token_count, head_width), bf16),
            pltpu.VMEM((blocks, *block), bf16),
            pltpu.VMEM((2, *block), bf16),
            pltpu.VMEM(block, bf16),
            pltpu.VMEM(block, bf16),
            pltpu.VMEM(block, bf16),
            pltpu.VMEM(block, bf16),
            dma((2, 2)),
            dma((2,)),
            dma((2,)),
        ]
        + [dma((steps,))] * 8
        + [dma((2, 2)), dma((blocks,)), dma((blocks - 1,)), dma((blocks,)), dma((3,)), dma((3,))],
        compiler_params=pltpu.CompilerParams(
            collective_id=0, has_side_effects=True, vmem_limit_bytes=60 * 1024 * 1024
        ),
        cost_estimate=pl.CostEstimate(
            flops=2 * steps * depth * width * (3 * hidden + 2 * half_tokens),
            bytes_accessed=6 * local * width * hidden * 2,
            transcendentals=steps * depth * quarter,
        ),
    )(picks, picks_t, row_gate, normed_all, heads_out, w_gate, w_up, w_down, w_out)


def body(
    n_expert,
    n_tensor,
    q_absorbed,
    kv_latent,
    w_values,
    w_out,
    layer_input,
    norm_gain,
    predicted,
    actual,
    gates,
    w_gate,
    w_up,
    w_down,
):
    local, slice_width, hidden = w_gate.shape
    experts = local * n_expert
    paired = n_tensor & (n_tensor - 1) == 0

    matches = predicted[:, None, :] == actual[:, :, None]
    matched = jnp.any(matches, axis=2)
    missed = jnp.sum(jnp.where(matched, 0.0, gates), axis=1)
    names = jnp.arange(experts, dtype=jnp.int32)
    gate_map = jnp.sum(
        jnp.where(actual[:, :, None] == names[None, None, :], gates[:, :, None], 0.0), axis=1
    )
    gate_terms, rest = [], gate_map
    for _ in range(3):
        term = lax.reduce_precision(rest, 8, 7)
        gate_terms.append(term.astype(jnp.bfloat16))
        rest = rest - term
    fill = -(kv_latent.shape[1] + 3 * experts) % 128
    gate_terms.append(jnp.zeros((gate_map.shape[0], fill), jnp.bfloat16))
    mixed = lax.all_gather(
        jnp.concatenate([kv_latent, *gate_terms], axis=1), "expert", axis=0, tiled=True
    )
    key_width = kv_latent.shape[1]
    kv_all = mixed[:, :key_width]
    gate_all = sum(
        mixed[:, key_width + i * experts : key_width + (i + 1) * experts].astype(jnp.float32)
        for i in range(3)
    )

    first_col = lax.axis_index("tensor") * slice_width
    features = layer_input.astype(jnp.float32)
    inverse = lax.rsqrt(jnp.mean(features * features, axis=1, keepdims=True) + EPS)
    mine = lax.dynamic_slice_in_dim(layer_input, first_col, slice_width, 1).astype(jnp.float32)
    gain_mine = lax.dynamic_slice_in_dim(norm_gain, first_col, slice_width, 0)
    normed = (mine * inverse * gain_mine).astype(jnp.bfloat16)
    normed_all = lax.all_gather(normed, "expert", axis=0, tiled=True)

    heads_out = attention(q_absorbed, kv_all, w_values)
    tokens = normed_all.shape[0]
    gate_here = lax.dynamic_slice_in_dim(
        gate_all, lax.axis_index("expert") * local, local, 1
    )
    if n_tensor == 4 and n_expert == 4 and hidden % 1024 == 0 and slice_width % 256 == 0:
        block = tokens // 4
        halves = [
            jnp.concatenate([part[:block], part[3 * block :], part[block : 3 * block]], axis=0)
            for part in (gate_here, normed_all)
        ]
        gate_halves = halves[0].reshape(2, 2 * block, local).transpose(0, 2, 1)
        depth = -(-2 * (CAP + CAP_C) // 16) * 16
        picks, row_gate = place_rows(gate_halves.reshape(2 * local, 2 * block), depth)
        attended, mixture = run_fused(
            picks,
            picks.transpose(0, 2, 1),
            row_gate[:, :, None],
            halves[1],
            heads_out,
            w_gate,
            w_up,
            w_down,
            w_out,
        )
        return (attended, mixture, missed)

    depth = n_expert * (CAP + CAP_C)
    picks, row_gate = place_rows(gate_here.T, depth)
    heads_all = lax.all_gather(heads_out, "expert", axis=0, tiled=True)
    outs = []
    for e in range(local):
        rows = jnp.dot(picks[e], normed_all, preferred_element_type=jnp.float32).astype(
            jnp.bfloat16
        )
        gate_part = jnp.dot(rows, w_gate[e], preferred_element_type=jnp.float32)
        up_part = jnp.dot(rows, w_up[e], preferred_element_type=jnp.float32)
        gate_part, up_part = gate_part.astype(jnp.bfloat16), up_part.astype(jnp.bfloat16)
        if paired:
            gate_share = reduce_halving(gate_part, 1, n_tensor)
            up_share = reduce_halving(up_part, 1, n_tensor)
        else:
            gate_share = lax.psum_scatter(gate_part, "tensor", scatter_dimension=1, tiled=True)
            up_share = lax.psum_scatter(up_part, "tensor", scatter_dimension=1, tiled=True)
            gate_share = gate_share.astype(jnp.float32)
            up_share = up_share.astype(jnp.float32)
        act_part = (jax.nn.silu(gate_share) * up_share).astype(jnp.bfloat16)
        if paired:
            act = gather_doubling(act_part, 1, n_tensor)
        else:
            act = lax.all_gather(act_part, "tensor", axis=1, tiled=True)
        out = jnp.dot(act, w_down[e], preferred_element_type=jnp.float32)
        outs.append((out * row_gate[e][:, None]).astype(jnp.bfloat16))
    partial_mix = lax.dot_general(
        picks.reshape(local * depth, tokens),
        jnp.concatenate(outs, axis=0),
        (((0,), (0,)), ((), ())),
        preferred_element_type=jnp.float32,
    ).astype(jnp.bfloat16)
    mixture = lax.psum_scatter(partial_mix, "expert", scatter_dimension=0, tiled=True)

    partial_cols = jnp.dot(heads_all, w_out, preferred_element_type=jnp.float32).astype(
        jnp.bfloat16
    )
    if paired and n_expert == n_tensor:
        summed = reduce_halving(partial_cols, 0, n_tensor).astype(jnp.bfloat16)
        attended = lax.ppermute(
            summed,
            ("expert", "tensor"),
            [
                (e * n_tensor + t, share_of(t, n_tensor) * n_tensor + e)
                for e in range(n_expert)
                for t in range(n_tensor)
            ],
        )
    else:
        partial_rows = lax.all_to_all(
            partial_cols, "expert", split_axis=0, concat_axis=1, tiled=True
        )
        attended = lax.psum_scatter(partial_rows, "tensor", scatter_dimension=1, tiled=True)
    return (attended, mixture, missed)


def solution(mesh):
    placed = (
        P(("group", "expert"), "tensor"),
        P(("group", "expert"), None),
        P("tensor", None, None),
        P("tensor", "expert"),
        P(("group", "expert"), None),
        P(),
        P(("group", "expert"), None),
        P(("group", "expert"), None),
        P(("group", "expert"), None),
        P("expert", "tensor", None),
        P("expert", "tensor", None),
        P("expert", None, "tensor"),
    )
    return jax.shard_map(
        functools.partial(body, mesh.shape["expert"], mesh.shape["tensor"]),
        mesh=mesh,
        in_specs=placed,
        out_specs=(
            P(("group", "expert"), "tensor"),
            P(("group", "expert"), "tensor"),
            P(("group", "expert")),
        ),
        check_vma=False,
    )
```

```python
import functools

import jax
import jax.numpy as jnp
from jax import lax
from jax.experimental import pallas as pl
from jax.experimental.pallas import tpu as pltpu
from jax.sharding import PartitionSpec as P

ROPE = 64
VDIM = 128
CAP = 80
CAP_C = 12


EPS = 1e-06
FLOOR = -1e30


def bits_of(count):
    return count.bit_length() - 1


def share_of(index, count):
    share = 0
    for bit in range(bits_of(count)):
        share = share * 2 + ((index >> bit) & 1)
    return share


def halve(part, dim, bit, count):
    own = (lax.axis_index("tensor") >> bit) & 1
    half = part.shape[dim] // 2
    send = lax.dynamic_slice_in_dim(part, (1 - own) * half, half, dim).astype(jnp.bfloat16)
    keep = lax.dynamic_slice_in_dim(part, own * half, half, dim).astype(jnp.float32)
    got = lax.ppermute(send, "tensor", [(i, i ^ (1 << bit)) for i in range(count)])
    return keep + got.astype(jnp.float32)


def reduce_halving(part, dim, count):
    for bit in range(bits_of(count)):
        part = halve(part, dim, bit, count)
    return part


def gather_doubling(part, dim, count):
    for bit in reversed(range(bits_of(count))):
        own = (lax.axis_index("tensor") >> bit) & 1
        got = lax.ppermute(part, "tensor", [(i, i ^ (1 << bit)) for i in range(count)])
        first = jnp.where(own == 0, part, got)
        second = jnp.where(own == 0, got, part)
        part = jnp.concatenate([first, second], axis=dim)
    return part


def place_rows(gate, depth):
    tokens = gate.shape[1]
    chosen = gate > 0.0
    order = jnp.arange(tokens, dtype=jnp.int32)
    upper = (order[:, None] <= order[None, :]).astype(jnp.bfloat16)
    place = jnp.dot(chosen.astype(jnp.bfloat16), upper, preferred_element_type=jnp.float32)
    place = jnp.where(chosen, place.astype(jnp.int32) - 1, -1)
    row_ids = jnp.arange(depth, dtype=jnp.int32)
    picks = place[:, None, :] == row_ids[None, :, None]
    row_gate = jnp.sum(jnp.where(picks, gate[:, None, :], 0.0), axis=2)
    return picks.astype(jnp.bfloat16), row_gate


def attention(q_absorbed, kv_all, w_values):
    token_count = q_absorbed.shape[0]
    heads_here = w_values.shape[0]
    latent_width = w_values.shape[1]
    key_width = kv_all.shape[1]
    scale = (VDIM + ROPE) ** (-0.5)
    queries = q_absorbed.reshape(token_count * heads_here, key_width)
    query_pos = jnp.repeat(
        lax.axis_index("expert") * token_count + jnp.arange(token_count, dtype=jnp.int32),
        heads_here,
    )
    scores = (
        lax.dot_general(
            queries, kv_all, (((1,), (1,)), ((), ())), preferred_element_type=jnp.float32
        )
        * scale
    )
    key_pos = jnp.arange(kv_all.shape[0], dtype=jnp.int32)
    visible = query_pos[:, None] >= key_pos[None, :]
    masked = jnp.where(visible, scores, FLOOR)
    largest = jnp.max(masked, axis=1)
    expo = jnp.where(visible, jnp.exp(masked - largest[:, None]), 0.0)
    denominator = jnp.sum(expo, axis=1)
    accum = jnp.dot(
        expo.astype(jnp.bfloat16), kv_all[:, :latent_width], preferred_element_type=jnp.float32
    )
    latent = (
        (accum / denominator[:, None])
        .astype(jnp.bfloat16)
        .reshape(token_count, heads_here, latent_width)
    )
    heads_out = jnp.einsum(
        "thc,hcv->thv", latent, w_values, preferred_element_type=jnp.float32
    ).astype(jnp.bfloat16)
    return heads_out.reshape(token_count, heads_here * w_values.shape[2])

MESH = pl.DeviceIdType.MESH


def fused_kernel(
    picks_ref,
    picks_t_ref,
    row_gate_ref,
    normed_ref,
    heads_ref,
    w_gate_ref,
    w_up_ref,
    w_down_ref,
    w_out_ref,
    attended_ref,
    mixture_ref,
    gate_buf,
    up_buf,
    down_buf,
    out_buf,
    rows,
    for_core,
    own_half,
    from_core,
    for_x,
    own_quarter,
    from_x,
    act,
    total,
    mix_out,
    mix_in,
    heads,
    cols_part,
    cols_core,
    cols_for_x,
    cols_from_x,
    cols_out,
    cols_in,
    weight_sem,
    down_sem,
    out_sem,
    core_send,
    core_recv,
    x_send,
    x_recv,
    act_x_send,
    act_x_recv,
    act_core_send,
    act_core_recv,
    mix_send,
    mix_recv,
    heads_send,
    heads_recv,
    cols_send,
    cols_recv,
):
    steps = picks_ref.shape[0]
    local = w_gate_ref.shape[0]
    blocks, token_count, _ = heads.shape
    quarter = own_quarter.shape[3]
    width = normed_ref.shape[1]
    tile = 256
    z = lax.axis_index("expert")
    me = lax.axis_index("tensor")
    core = lax.rem(me, 2)
    side = me // 2
    core_peer = side * 2 + 1 - core
    x_peer = (1 - side) * 2 + core
    mine = core * 2 + side
    stays = (mine == z) & (z == me)

    def remote(src, dst, send, recv, peer):
        return pltpu.make_async_remote_copy(
            src_ref=src,
            dst_ref=dst,
            send_sem=send,
            recv_sem=recv,
            device_id=peer,
            device_id_type=MESH,
        )

    def weight_copies(s):
        slot, e = lax.rem(s, 2), lax.rem(s, local)
        return (
            pltpu.make_async_copy(w_gate_ref.at[e], gate_buf.at[slot], weight_sem.at[0, slot]),
            pltpu.make_async_copy(w_up_ref.at[e], up_buf.at[slot], weight_sem.at[1, slot]),
        )

    def down_copy(s):
        slot, e = lax.rem(s, 2), lax.rem(s, local)
        return pltpu.make_async_copy(w_down_ref.at[e], down_buf.at[slot], down_sem.at[slot])

    def out_copy(j):
        slot = lax.rem(j, 2)
        cols = pl.ds(pl.multiple_of(j * tile, tile), tile)
        return pltpu.make_async_copy(w_out_ref.at[:, cols], out_buf.at[slot], out_sem.at[slot])

    def core_copy(s):
        return remote(
            for_core.at[lax.rem(s, 2)],
            from_core.at[s],
            core_send.at[s],
            core_recv.at[s],
            {"tensor": core_peer},
        )

    def x_copy(s):
        return remote(
            for_x.at[lax.rem(s, 2)], from_x.at[s], x_send.at[s], x_recv.at[s], {"tensor": x_peer}
        )

    def act_x_copy(s):
        part = act.at[s, mine]
        return remote(part, part, act_x_send.at[s], act_x_recv.at[s], {"tensor": x_peer})

    def act_core_copy(s):
        part = act.at[s, pl.ds(core * 2, 2)]
        return remote(part, part, act_core_send.at[s], act_core_recv.at[s], {"tensor": core_peer})

    def heads_copy(k):
        peer = lax.rem(z + k, blocks)
        return remote(
            heads_ref, heads.at[z], heads_send.at[k - 1], heads_recv.at[z], {"expert": peer}
        )

    def heads_arrival(k):
        source = lax.rem(z + k, blocks)
        return remote(
            heads_ref, heads.at[source], heads_send.at[k - 1], heads_recv.at[source], {"expert": source}
        )

    def cols_core_copy():
        return remote(
            cols_part.at[pl.ds((1 - core) * 2, 2)],
            cols_core,
            cols_send.at[0],
            cols_recv.at[0],
            {"tensor": core_peer},
        )

    def cols_x_copy():
        return remote(
            cols_for_x, cols_from_x, cols_send.at[1], cols_recv.at[1], {"tensor": x_peer}
        )

    def cols_final_copy():
        return remote(
            cols_out,
            cols_in,
            cols_send.at[2],
            cols_recv.at[2],
            {"expert": mine, "tensor": z},
        )

    def mix_target(half, i):
        return half + i * (blocks - 1 - 2 * half)

    def mix_copy(half, i):
        return remote(
            mix_out.at[half, i],
            mix_in.at[z],
            mix_send.at[half, i],
            mix_recv.at[z],
            {"expert": mix_target(half, i)},
        )

    def mix_arrival(source):
        return remote(
            mix_out.at[0, 0],
            mix_in.at[source],
            mix_send.at[0, 0],
            mix_recv.at[source],
            {"expert": source},
        )

    for copy in weight_copies(0):
        copy.start()
    down_copy(0).start()
    barrier = pltpu.get_barrier_semaphore()

    def greet(peer):
        pl.semaphore_signal(barrier, inc=1, device_id=peer, device_id_type=MESH)

    greet({"tensor": core_peer})
    greet({"tensor": x_peer})
    for k in range(1, blocks):
        greet({"expert": lax.rem(z + k, blocks)})

    @pl.when(jnp.logical_not(stays))
    def _():
        greet({"expert": mine, "tensor": z})
        greet({"expert": me, "tensor": lax.rem(z, 2) * 2 + z // 2})

    @pl.when(stays)
    def _():
        pl.semaphore_wait(barrier, 1 + blocks)

    @pl.when(jnp.logical_not(stays))
    def _():
        pl.semaphore_wait(barrier, 3 + blocks)

    for k in range(1, blocks):
        heads_copy(k).start()
    heads[z] = heads_ref[...]

    def multiply(s):
        slot = lax.rem(s, 2)
        half = s // local
        outer = pl.ds(pl.multiple_of(half * token_count, token_count), token_count)
        inner = pl.ds(
            pl.multiple_of((blocks - 1 - half) * token_count, token_count), token_count
        )

        @pl.when(s + 1 < steps)
        def _():
            for copy in weight_copies(s + 1):
                copy.start()

        @pl.loop(0, width // tile)
        def _(j):
            cols = pl.ds(pl.multiple_of(j * tile, tile), tile)
            rows[:, cols] = (
                jnp.dot(
                    picks_ref[s, :, :token_count],
                    normed_ref[outer, cols],
                    preferred_element_type=jnp.float32,
                )
                + jnp.dot(
                    picks_ref[s, :, token_count:],
                    normed_ref[inner, cols],
                    preferred_element_type=jnp.float32,
                )
            ).astype(jnp.bfloat16)

        for copy in weight_copies(s):
            copy.wait()
        for core_half, target in ((1 - core, for_core), (core, own_half)):
            for k, x_half in enumerate((1 - side, side)):
                first = pl.multiple_of((core_half * 2 + x_half) * quarter, quarter)
                cols = pl.ds(first, quarter)
                for m, buf in enumerate((gate_buf, up_buf)):
                    target[slot, 2 * k + m] = jnp.dot(
                        rows[...], buf[slot, :, cols], preferred_element_type=jnp.float32
                    ).astype(jnp.bfloat16)
            if target is for_core:
                core_copy(s).start()

    def add_core(s):
        slot = lax.rem(s, 2)
        core_copy(s).wait()
        for k in range(2):
            for_x[slot, k] = (
                own_half[slot, k].astype(jnp.float32) + from_core[s, k].astype(jnp.float32)
            ).astype(jnp.bfloat16)
        x_copy(s).start()
        for k in range(2):
            own_quarter[slot, k] = own_half[slot, 2 + k].astype(jnp.float32) + from_core[
                s, 2 + k
            ].astype(jnp.float32)

    def activate(s):
        slot = lax.rem(s, 2)
        x_copy(s).wait()
        gate = own_quarter[slot, 0] + from_x[s, 0].astype(jnp.float32)
        up = own_quarter[slot, 1] + from_x[s, 1].astype(jnp.float32)
        act[s, mine] = (gate / (1.0 + jnp.exp(-gate)) * up).astype(jnp.bfloat16)
        act_x_copy(s).start()

    def pass_on(s):
        act_x_copy(s).wait()
        act_core_copy(s).start()

    def project(s):
        slot = lax.rem(s, 2)

        @pl.when(s + 1 < steps)
        def _():
            down_copy(s + 1).start()

        @pl.when(lax.rem(s, local) == 0)
        def _():
            total[...] = jnp.zeros_like(total)

        act_core_copy(s).wait()
        down_copy(s).wait()

        @pl.loop(0, width // tile)
        def _(j):
            cols = pl.ds(pl.multiple_of(j * tile, tile), tile)
            out = jnp.zeros((act.shape[2], tile), jnp.float32)
            for q in range(act.shape[1]):
                out += jnp.dot(
                    act[s, q],
                    down_buf[slot, q * quarter : (q + 1) * quarter, cols],
                    preferred_element_type=jnp.float32,
                )
            out = (out * row_gate_ref[s]).astype(jnp.bfloat16)
            total[:, cols] += jnp.dot(picks_t_ref[s], out, preferred_element_type=jnp.float32)

        @pl.when(lax.rem(s, local) == local - 1)
        def _():
            half = s // local
            for i in range(2):
                mix_out[half, i] = total[i * token_count : (i + 1) * token_count, :].astype(
                    jnp.bfloat16
                )

                @pl.when(mix_target(half, i) != z)
                def _():
                    mix_copy(half, i).start()

                @pl.when(mix_target(half, i) == z)
                def _():
                    mix_in[z] = mix_out[half, i]

    def multiply_heads():
        out_copy(0).start()
        for k in range(1, blocks):
            heads_copy(k).wait_send()
            heads_arrival(k).wait_recv()

        @pl.loop(0, width // tile)
        def _(j):
            @pl.when(j + 1 < width // tile)
            def _():
                out_copy(j + 1).start()

            out_copy(j).wait()
            cols = pl.ds(pl.multiple_of(j * tile, tile), tile)
            for b in range(blocks // 2):
                part = heads[2 * b : 2 * b + 2].reshape(2 * token_count, heads.shape[2])
                part = jnp.dot(
                    part, out_buf[lax.rem(j, 2)], preferred_element_type=jnp.float32
                ).astype(jnp.bfloat16)
                cols_part[2 * b : 2 * b + 2, :, cols] = part.reshape(2, token_count, tile)

        cols_core_copy().start()

    def add_cols_core():
        cols_core_copy().wait()
        cols_for_x[...] = (
            cols_part[core * 2 + 1 - side].astype(jnp.float32)
            + cols_core[1 - side].astype(jnp.float32)
        ).astype(jnp.bfloat16)
        cols_x_copy().start()

    def add_cols_x():
        cols_x_copy().wait()
        cols_out[...] = (
            cols_part[mine].astype(jnp.float32)
            + cols_core[side].astype(jnp.float32)
            + cols_from_x[...].astype(jnp.float32)
        ).astype(jnp.bfloat16)

        @pl.when(jnp.logical_not(stays))
        def _():
            cols_final_copy().start()

    @pl.loop(0, steps + 4)
    def _(step):
        @pl.when((step >= 1) & (step < steps + 1))
        def _():
            add_core(step - 1)

        @pl.when(step < steps)
        def _():
            multiply(step)

        @pl.when((step >= 2) & (step < steps + 2))
        def _():
            activate(step - 2)

        @pl.when((step >= 3) & (step < steps + 3))
        def _():
            pass_on(step - 3)

        @pl.when(step == steps - 2)
        def _():
            add_cols_core()

        @pl.when(step == steps - 1)
        def _():
            add_cols_x()

        @pl.when(step >= 4)
        def _():
            project(step - 4)

        @pl.when(step == steps - 3)
        def _():
            multiply_heads()

    @pl.when(jnp.logical_not(stays))
    def _():
        cols_final_copy().wait()
        attended_ref[...] = cols_in[...].astype(jnp.float32)

    @pl.when(stays)
    def _():
        attended_ref[...] = cols_out[...].astype(jnp.float32)

    for half in range(2):
        for i in range(2):

            @pl.when(mix_target(half, i) != z)
            def _():
                mix_copy(half, i).wait_send()

    for source in range(blocks):

        @pl.when(z != source)
        def _():
            mix_arrival(source).wait_recv()

    mixed = mix_in[0].astype(jnp.float32)
    for source in range(1, blocks):
        mixed += mix_in[source].astype(jnp.float32)
    mixture_ref[...] = mixed


def run_fused(picks, picks_t, row_gate, normed_all, heads_out, w_gate, w_up, w_down, w_out):
    steps, depth, half_tokens = picks.shape
    local, width, hidden = w_gate.shape
    token_count, head_width = heads_out.shape
    blocks = 4
    quarter = hidden // 4
    bf16, f32 = jnp.bfloat16, jnp.float32
    dma = pltpu.SemaphoreType.DMA
    vmem = pl.BlockSpec(memory_space=pltpu.VMEM)
    hbm = pl.BlockSpec(memory_space=pl.ANY)
    block = (token_count, width)
    return pl.pallas_call(
        fused_kernel,
        out_shape=[jax.ShapeDtypeStruct(block, f32)] * 2,
        in_specs=[vmem] * 5 + [hbm] * 4,
        out_specs=[vmem] * 2,
        scratch_shapes=[
            pltpu.VMEM((2, width, hidden), bf16),
            pltpu.VMEM((2, width, hidden), bf16),
            pltpu.VMEM((2, hidden, width), bf16),
            pltpu.VMEM((2, head_width, 256), bf16),
            pltpu.VMEM((depth, width), bf16),
            pltpu.VMEM((2, 4, depth, quarter), bf16),
            pltpu.VMEM((2, 4, depth, quarter), bf16),
            pltpu.VMEM((steps, 4, depth, quarter), bf16),
            pltpu.VMEM((2, 2, depth, quarter), bf16),
            pltpu.VMEM((2, 2, depth, quarter), f32),
            pltpu.VMEM((steps, 2, depth, quarter), bf16),
            pltpu.VMEM((steps, 4, depth, quarter), bf16),
            pltpu.VMEM((half_tokens, width), f32),
            pltpu.VMEM((2, 2, *block), bf16),
            pltpu.VMEM((blocks, *block), bf16),
            pltpu.VMEM((blocks, token_count, head_width), bf16),
            pltpu.VMEM((blocks, *block), bf16),
            pltpu.VMEM((2, *block), bf16),
            pltpu.VMEM(block, bf16),
            pltpu.VMEM(block, bf16),
            pltpu.VMEM(block, bf16),
            pltpu.VMEM(block, bf16),
            dma((2, 2)),
            dma((2,)),
            dma((2,)),
        ]
        + [dma((steps,))] * 8
        + [dma((2, 2)), dma((blocks,)), dma((blocks - 1,)), dma((blocks,)), dma((3,)), dma((3,))],
        compiler_params=pltpu.CompilerParams(
            collective_id=0, has_side_effects=True, vmem_limit_bytes=60 * 1024 * 1024
        ),
        cost_estimate=pl.CostEstimate(
            flops=2 * steps * depth * width * (3 * hidden + 2 * half_tokens),
            bytes_accessed=6 * local * width * hidden * 2,
            transcendentals=steps * depth * quarter,
        ),
    )(picks, picks_t, row_gate, normed_all, heads_out, w_gate, w_up, w_down, w_out)


def body(
    n_expert,
    n_tensor,
    q_absorbed,
    kv_latent,
    w_values,
    w_out,
    layer_input,
    norm_gain,
    predicted,
    actual,
    gates,
    w_gate,
    w_up,
    w_down,
):
    local, slice_width, hidden = w_gate.shape
    experts = local * n_expert
    paired = n_tensor & (n_tensor - 1) == 0

    matches = predicted[:, None, :] == actual[:, :, None]
    matched = jnp.any(matches, axis=2)
    missed = jnp.sum(jnp.where(matched, 0.0, gates), axis=1)
    names = jnp.arange(experts, dtype=jnp.int32)
    gate_map = jnp.sum(
        jnp.where(actual[:, :, None] == names[None, None, :], gates[:, :, None], 0.0), axis=1
    )
    gate_terms, rest = [], gate_map
    for _ in range(3):
        term = lax.reduce_precision(rest, 8, 7)
        gate_terms.append(term.astype(jnp.bfloat16))
        rest = rest - term
    fill = -(kv_latent.shape[1] + 3 * experts) % 128
    gate_terms.append(jnp.zeros((gate_map.shape[0], fill), jnp.bfloat16))
    mixed = jnp.concatenate([kv_latent, *gate_terms], axis=1)
    if n_tensor % 2 == 0:
        own = lax.axis_index("tensor") & 1
        half_rows = mixed.shape[0] // 2
        part = lax.dynamic_slice_in_dim(mixed, own * half_rows, half_rows, 0)
        part = lax.all_gather(part, "expert", axis=0, tiled=False)
        got = lax.ppermute(part, "tensor", [(i, i ^ 1) for i in range(n_tensor)])
        mixed = jnp.concatenate(
            [jnp.where(own == 0, part, got), jnp.where(own == 0, got, part)], axis=1
        ).reshape(-1, mixed.shape[1])
    else:
        mixed = lax.all_gather(mixed, "expert", axis=0, tiled=True)
    key_width = kv_latent.shape[1]
    kv_all = mixed[:, :key_width]
    gate_all = sum(
        mixed[:, key_width + i * experts : key_width + (i + 1) * experts].astype(jnp.float32)
        for i in range(3)
    )

    first_col = lax.axis_index("tensor") * slice_width
    features = layer_input.astype(jnp.float32)
    inverse = lax.rsqrt(jnp.mean(features * features, axis=1, keepdims=True) + EPS)
    mine = lax.dynamic_slice_in_dim(layer_input, first_col, slice_width, 1).astype(jnp.float32)
    gain_mine = lax.dynamic_slice_in_dim(norm_gain, first_col, slice_width, 0)
    normed = (mine * inverse * gain_mine).astype(jnp.bfloat16)
    normed_all = lax.all_gather(normed, "expert", axis=0, tiled=True)

    heads_out = attention(q_absorbed, kv_all, w_values)
    tokens = normed_all.shape[0]
    gate_here = lax.dynamic_slice_in_dim(
        gate_all, lax.axis_index("expert") * local, local, 1
    )
    if n_tensor == 4 and n_expert == 4 and hidden % 1024 == 0 and slice_width % 256 == 0:
        block = tokens // 4
        gate_halves = jnp.concatenate(
            [gate_here[:block], gate_here[3 * block :], gate_here[block : 3 * block]], axis=0
        )
        gate_halves = gate_halves.reshape(2, 2 * block, local).transpose(0, 2, 1)
        depth = -(-2 * (CAP + CAP_C) // 16) * 16
        picks, row_gate = place_rows(gate_halves.reshape(2 * local, 2 * block), depth)
        attended, mixture = run_fused(
            picks,
            picks.transpose(0, 2, 1),
            row_gate[:, :, None],
            normed_all,
            heads_out,
            w_gate,
            w_up,
            w_down,
            w_out,
        )
        return (attended.astype(jnp.bfloat16), mixture.astype(jnp.bfloat16), missed)

    depth = n_expert * (CAP + CAP_C)
    picks, row_gate = place_rows(gate_here.T, depth)
    heads_all = lax.all_gather(heads_out, "expert", axis=0, tiled=True)
    outs = []
    for e in range(local):
        rows = jnp.dot(picks[e], normed_all, preferred_element_type=jnp.float32).astype(
            jnp.bfloat16
        )
        gate_part = jnp.dot(rows, w_gate[e], preferred_element_type=jnp.float32)
        up_part = jnp.dot(rows, w_up[e], preferred_element_type=jnp.float32)
        gate_part, up_part = gate_part.astype(jnp.bfloat16), up_part.astype(jnp.bfloat16)
        if paired:
            gate_share = reduce_halving(gate_part, 1, n_tensor)
            up_share = reduce_halving(up_part, 1, n_tensor)
        else:
            gate_share = lax.psum_scatter(gate_part, "tensor", scatter_dimension=1, tiled=True)
            up_share = lax.psum_scatter(up_part, "tensor", scatter_dimension=1, tiled=True)
            gate_share = gate_share.astype(jnp.float32)
            up_share = up_share.astype(jnp.float32)
        act_part = (jax.nn.silu(gate_share) * up_share).astype(jnp.bfloat16)
        if paired:
            act = gather_doubling(act_part, 1, n_tensor)
        else:
            act = lax.all_gather(act_part, "tensor", axis=1, tiled=True)
        out = jnp.dot(act, w_down[e], preferred_element_type=jnp.float32)
        outs.append((out * row_gate[e][:, None]).astype(jnp.bfloat16))
    partial_mix = lax.dot_general(
        picks.reshape(local * depth, tokens),
        jnp.concatenate(outs, axis=0),
        (((0,), (0,)), ((), ())),
        preferred_element_type=jnp.float32,
    ).astype(jnp.bfloat16)
    mixture = lax.psum_scatter(partial_mix, "expert", scatter_dimension=0, tiled=True)

    partial_cols = jnp.dot(heads_all, w_out, preferred_element_type=jnp.float32).astype(
        jnp.bfloat16
    )
    if paired and n_expert == n_tensor:
        summed = reduce_halving(partial_cols, 0, n_tensor).astype(jnp.bfloat16)
        attended = lax.ppermute(
            summed,
            ("expert", "tensor"),
            [
                (e * n_tensor + t, share_of(t, n_tensor) * n_tensor + e)
                for e in range(n_expert)
                for t in range(n_tensor)
            ],
        )
    else:
        partial_rows = lax.all_to_all(
            partial_cols, "expert", split_axis=0, concat_axis=1, tiled=True
        )
        attended = lax.psum_scatter(partial_rows, "tensor", scatter_dimension=1, tiled=True)
    return (attended, mixture, missed)


def solution(mesh):
    placed = (
        P(("group", "expert"), "tensor"),
        P(("group", "expert"), None),
        P("tensor", None, None),
        P("tensor", "expert"),
        P(("group", "expert"), None),
        P(),
        P(("group", "expert"), None),
        P(("group", "expert"), None),
        P(("group", "expert"), None),
        P("expert", "tensor", None),
        P("expert", "tensor", None),
        P("expert", None, "tensor"),
    )
    return jax.shard_map(
        functools.partial(body, mesh.shape["expert"], mesh.shape["tensor"]),
        mesh=mesh,
        in_specs=placed,
        out_specs=(
            P(("group", "expert"), "tensor"),
            P(("group", "expert"), "tensor"),
            P(("group", "expert")),
        ),
        check_vma=False,
    )
```
